256 devices in a mesh: diag: 32 (over z, y_hi, core), off: 8 (over y_lo, x).
Axes of the slice: x: 4, y: 4 (y_hi: 2, y_lo: 2; y = y_hi * 2 + y_lo), z: 8, core: 2. Of those that a mesh axis runs over, the one named last changes fastest.
Arguments:
- vectors: bfloat16 [16, 524288], P(None, ('diag', 'off')), may hold values from -6 to 6
- tile_blocks: bfloat16 [81920, 128, 128], P(('diag', 'off')), may hold values from -0.078125 to 0.078125
- tile_index: int32 [81920, 2], P(('diag', 'off')), may hold values from 0 to 127
- tile_live: int32 [81920, 2], P(('diag', 'off')), may hold values from 32 to 128
- tile_count: int32 [256], P(('diag', 'off')), may hold values from 40 to 320, as said below
Outputs:
- image: float32 [16, 524288], P(None, ('diag', 'off'))
The draws below stay inside these ranges and needn't reach their ends.
Inputs may be any that keep to these rules, and one draw needn't show every extreme that they name: `tile_count`: the live slots of a device are its first ones; some device has all 320 slots live and another only 40.
All inputs are finite; a program needn't handle non-finite values.
Results may differ from the reference program's by a relative error of at most 0.0003.
Values may be sent and summed in bfloat16 or wider, within the bound.
No kernel may reach another device: no remote copies, remote signals or barrier semaphores. Data moves between devices by JAX's collectives and lax.ppermute only.
A program may use at most 64 MiB of HBM per device.

```python
import jax
import jax.numpy as jnp
from jax import lax

NVEC = 16
TILE = 128
TILES_DEV = 320
NBLK = 128
BASIS = 524288
GRID = 256
SLOTS = 81920
N_DIAG = 32
N_OFF = 8


def draw_tile_count(key, part):
    key = jax.random.fold_in(key, 5)
    first_key, second_key, third_key = jax.random.split(key, 3)
    lowest = TILES_DEV // 8
    raw_draw = jax.random.randint(first_key, (GRID,), 0, TILES_DEV + 1)
    counts = lowest + raw_draw * raw_draw * (TILES_DEV - lowest) // (TILES_DEV * TILES_DEV)
    chosen = jax.random.randint(second_key, (), 0, GRID)
    other = (chosen + 1 + jax.random.randint(third_key, (), 0, GRID - 1)) % GRID
    positions = jnp.arange(GRID)
    counts = jnp.where(positions == chosen, TILES_DEV, counts)
    counts = jnp.where(positions == other, lowest, counts)
    return counts.astype(jnp.int32)


def with_ends(array, own_key, least, largest):
    longest = array.shape.index(max(array.shape))
    spots = []
    for shift in (0, 1):
        where = [jax.random.randint(jax.random.fold_in(own_key, axis), (), 0, length) for axis, length in enumerate(array.shape)]
        where[longest] = (where[longest] + shift) % array.shape[longest]
        spots.append(tuple(where))
    return array.at[spots[0]].set(least).at[spots[1]].set(largest)


def shard_levels(rng, dims, shards, low, high):
    factor_of, own = 1.0, jax.random.fold_in(rng, 6)
    for axis_at, shards_of in shards:
        heights = jnp.exp(jax.random.uniform(jax.random.fold_in(own, axis_at), (shards_of,), jnp.float32, low / len(shards), high / len(shards)))
        factor_of = factor_of * jnp.repeat(heights, dims[axis_at] // shards_of).reshape([-1 if axis == axis_at else 1 for axis in range(len(dims))])
    return factor_of


def centred(stream_key, shape, scale, limit, cuts=(), held_as=jnp.bfloat16):
    values = jax.random.normal(stream_key, shape, jnp.float32) * scale
    if len(cuts) > 0:
        values = shard_levels(stream_key, shape, cuts, -0.22, 0.18) * values
    return jnp.clip(values, min=-limit, max=limit).astype(held_as)


def setup_inputs(seed: int = 0) -> dict:
    key_list = jax.random.split(jax.random.key(seed), 6)
    return {
        "vectors": centred(key_list[0], (NVEC, BASIS), 1.0, 6.0, ((1, 256),)),
        "tile_blocks": centred(key_list[1], (SLOTS, TILE, TILE), (2 * N_OFF * TILES_DEV * TILE // NBLK) ** -0.5, 0.078125, ((0, 256),)),
        "tile_index": with_ends(jax.random.randint(key_list[2], (SLOTS, 2), 0, NBLK), jax.random.fold_in(key_list[2], 1), 0, NBLK - 1).astype(jnp.int32),
        "tile_live": with_ends(jax.random.randint(key_list[3], (SLOTS, 2), TILE // 4, TILE + 1), jax.random.fold_in(key_list[3], 1), TILE // 4, TILE).astype(jnp.int32),
        "tile_count": draw_tile_count(jax.random.fold_in(key_list[5], 71), 0),
    }


def reference(vectors, tile_blocks, tile_index, tile_live, tile_count):
    grid_total = N_DIAG * N_OFF
    all_blocks = N_DIAG * NBLK
    x_all = vectors.astype(jnp.float32).reshape(NVEC, all_blocks, TILE)
    within = jnp.arange(TILE, dtype=jnp.int32)
    slot_ids = jnp.arange(TILES_DEV, dtype=jnp.int32)
    stored = tile_blocks.reshape(grid_total, TILES_DEV, TILE, TILE)
    indices = tile_index.reshape(grid_total, TILES_DEV, 2)
    lives = tile_live.reshape(grid_total, TILES_DEV, 2)
    devices = jnp.arange(grid_total, dtype=jnp.int32)

    def device_step(carry, inputs):
        blocks, index_part, live_part, live_count, device = inputs
        grid_row = device // N_OFF
        grid_col = device % N_OFF
        col_segment = (grid_row + grid_col) % N_DIAG
        row_global = (grid_row * NBLK + index_part[:, 0]).astype(jnp.int32)
        col_global = (col_segment * NBLK + index_part[:, 1]).astype(jnp.int32)
        alive = slot_ids < live_count
        row_keep = ((within[None, :] < live_part[:, 0:1]) & alive[:, None]).astype(jnp.float32)
        col_keep = (within[None, :] < live_part[:, 1:2]).astype(jnp.float32)
        dense = blocks.astype(jnp.float32)
        from_cols = x_all[:, col_global] * col_keep[None]
        forward = jnp.einsum('ktj,tij->kti', from_cols, dense) * row_keep[None]
        from_rows = x_all[:, row_global] * row_keep[None]
        backward = jnp.einsum('kti,tij->ktj', from_rows, dense) * col_keep[None]
        carry = carry.at[:, row_global].add(forward)
        carry = carry.at[:, col_global].add(backward)
        return carry, None

    start = jnp.zeros((NVEC, all_blocks, TILE), jnp.float32)
    total, _ = lax.scan(device_step, start, (stored, indices, lives, tile_count, devices))
    return total.reshape(NVEC, all_blocks * TILE)
```

```python
import functools

import jax
import jax.numpy as jnp
from jax import lax
from jax.experimental import pallas as pl
from jax.experimental.pallas import tpu as pltpu
from jax.sharding import PartitionSpec as P

AXES = ("diag", "off")
TILE = 128
UNROLL = 32
VMEM = pl.BlockSpec(memory_space=pltpu.VMEM)
SMEM = pl.BlockSpec(memory_space=pltpu.SMEM)


def params(mib):
    return pltpu.CompilerParams(vmem_limit_bytes=mib * 2**20)


def block_at(ref, block, per_part):
    lanes = pl.multiple_of(lax.rem(block, per_part) * TILE, TILE)
    return ref.at[lax.div(block, per_part), :, pl.ds(lanes, TILE)]


def quantized(source, target, part, per_part):
    nvecs = source.shape[1]
    lane = lax.broadcasted_iota(jnp.int32, (nvecs, TILE), 1)
    exponents = jnp.zeros((nvecs, TILE), jnp.int32)
    for block in range(per_part):
        values = source[part, :, block * TILE : (block + 1) * TILE]
        largest = jnp.max(jnp.abs(values), axis=1, keepdims=True)
        power = jnp.floor(jnp.log2(jnp.maximum(largest, 2.0**-100)))
        scaled = jnp.round(values * jnp.exp2(14.0 - power))
        scaled = jnp.clip(scaled, -32767.0, 32767.0).astype(jnp.int32)
        target[part, :, block * TILE : (block + 1) * TILE] = scaled.astype(jnp.int16)
        exponents = jnp.where(lane == block, power.astype(jnp.int32), exponents)
    target[part, :, per_part * TILE :] = exponents.astype(jnp.int16)


def restored(source, part, block, per_part):
    exponents = source[part, :, per_part * TILE :].astype(jnp.int32).astype(jnp.float32)
    scale = jnp.exp2(exponents[:, block : block + 1] - 14.0)
    values = source[part, :, block * TILE : (block + 1) * TILE]
    return values.astype(jnp.int32).astype(jnp.float32) * scale


def tiles_kernel(transposed, per_part, meta, count, x_ref, tiles_ref, out_ref, acc_ref=None):
    total = out_ref if acc_ref is None else acc_ref
    live = count[0]
    nvecs = x_ref.shape[1]
    total[...] = jnp.zeros_like(total)
    lane = lax.broadcasted_iota(jnp.int32, (nvecs, TILE), 1)

    def group(index, carry):
        products = []
        for step in range(UNROLL):
            slot = index * UNROLL + step
            code = meta[slot]
            alive = slot < live
            rows = jnp.where(alive, (code >> 14) & 0xFF, 0)
            columns = jnp.where(alive, (code >> 22) & 0xFF, 0)
            row_block, column_block = code & 0x7F, (code >> 7) & 0x7F
            if transposed:
                taken, given, source, target = columns, rows, column_block, row_block
            else:
                taken, given, source, target = rows, columns, row_block, column_block
            x = block_at(x_ref, source, per_part)[...]
            x = jnp.where(lane < taken, x.astype(jnp.float32), 0.0).astype(jnp.bfloat16)
            dims = (((1,), (1 if transposed else 0,)), ((), ()))
            product = lax.dot_general(x, tiles_ref[slot], dims, preferred_element_type=jnp.float32)
            products.append((target, jnp.where(lane < given, product, 0.0)))
        for target, product in products:
            block_at(total, target, per_part)[...] += product
        return carry

    lax.fori_loop(0, lax.div(live + UNROLL - 1, UNROLL), group, 0)
    if acc_ref is not None:
        def part_out(part, carry):
            quantized(acc_ref, out_ref, part, per_part)
            return carry

        lax.fori_loop(0, out_ref.shape[0], part_out, 0)


def column_partials(meta, count, x, tiles):
    parts, nvecs, width = x.shape
    per_part = width // TILE
    return pl.pallas_call(
        functools.partial(tiles_kernel, False, per_part),
        out_shape=jax.ShapeDtypeStruct((parts, nvecs, width + TILE), jnp.int16),
        in_specs=[SMEM, SMEM, VMEM, VMEM],
        out_specs=VMEM,
        scratch_shapes=[pltpu.VMEM((parts, nvecs, width), jnp.float32)],
        compiler_params=params(32),
        cost_estimate=pl.CostEstimate(flops=10**9, bytes_accessed=12 * 2**20, transcendentals=0),
    )(meta, count, x, tiles)


def row_partials(meta, count, x, tiles):
    parts, nvecs, width = x.shape
    per_part = width // TILE
    return pl.pallas_call(
        functools.partial(tiles_kernel, True, per_part),
        out_shape=jax.ShapeDtypeStruct((parts, nvecs, width), jnp.float32),
        in_specs=[SMEM, SMEM, VMEM, VMEM],
        out_specs=VMEM,
        compiler_params=params(32),
        cost_estimate=pl.CostEstimate(flops=10**9, bytes_accessed=12 * 2**20, transcendentals=0),
    )(meta, count, x, tiles)


def joined_kernel(per_part, rows_ref, arrived_ref, out_ref, total_ref):
    def one_part(part, carry):
        for block in range(per_part):
            lanes = slice(block * TILE, (block + 1) * TILE)
            total_ref[part, :, lanes] = rows_ref[part, :, lanes] + restored(arrived_ref, part, block, per_part)
        quantized(total_ref, out_ref, part, per_part)
        return carry

    lax.fori_loop(0, out_ref.shape[0], one_part, 0)


def joined(rows, arrived):
    parts, nvecs, width = rows.shape
    return pl.pallas_call(
        functools.partial(joined_kernel, width // TILE),
        out_shape=jax.ShapeDtypeStruct(arrived.shape, jnp.int16),
        in_specs=[VMEM, VMEM],
        out_specs=VMEM,
        scratch_shapes=[pltpu.VMEM((parts, nvecs, width), jnp.float32)],
        compiler_params=params(16),
    )(rows, arrived)


def summed_kernel(per_part, parts_ref, out_ref):
    for block in range(per_part):
        total = restored(parts_ref, 0, block, per_part)
        for part in range(1, parts_ref.shape[0]):
            total = total + restored(parts_ref, part, block, per_part)
        out_ref[:, block * TILE : (block + 1) * TILE] = total


def summed(parts):
    nvecs, width = parts.shape[1], parts.shape[2] - TILE
    return pl.pallas_call(
        functools.partial(summed_kernel, width // TILE),
        out_shape=jax.ShapeDtypeStruct((nvecs, width), jnp.float32),
        in_specs=[VMEM],
        out_specs=VMEM,
        compiler_params=params(16),
    )(parts)


def per_device(vectors, tile_blocks, tile_index, tile_live, tile_count):
    n_diag, n_off = lax.axis_size("diag"), lax.axis_size("off")
    fetch = [
        (((a + b) % n_diag) * n_off + b, a * n_off + b) for a in range(n_diag) for b in range(n_off)
    ]
    meta = tile_index[:, 0] | (tile_index[:, 1] << 7) | (tile_live[:, 0] << 14) | (tile_live[:, 1] << 22)
    copies = jnp.broadcast_to(vectors[None], (n_off, *vectors.shape))
    x_rows = lax.all_to_all(copies, "off", 0, 0)
    x_columns = lax.ppermute(x_rows, AXES, fetch)
    sent = column_partials(meta, tile_count, x_rows, tile_blocks)
    arrived = lax.ppermute(sent, AXES, [(there, here) for here, there in fetch])
    rows = row_partials(meta, tile_count, x_columns, tile_blocks)
    return summed(lax.all_to_all(joined(rows, arrived), "off", 0, 0))


def solution(mesh):
    placed = (
        P(None, AXES),
        P(AXES, None, None),
        P(AXES, None),
        P(AXES, None),
        P(AXES),
    )
    return jax.shard_map(
        per_device, mesh=mesh, in_specs=placed, out_specs=P(None, AXES), check_vma=False
    )
```

```python
import functools

import jax
import jax.numpy as jnp
from jax import lax
from jax.experimental import pallas as pl
from jax.experimental.pallas import tpu as pltpu
from jax.sharding import PartitionSpec as P

AXES = ("diag", "off")
TILE = 128
UNROLL = 32
VMEM = pl.BlockSpec(memory_space=pltpu.VMEM)
HBM = pl.BlockSpec(memory_space=pltpu.HBM)
SMEM = pl.BlockSpec(memory_space=pltpu.SMEM)


def params(mib):
    return pltpu.CompilerParams(vmem_limit_bytes=mib * 2**20)


def block_at(ref, block, per_part):
    lanes = pl.multiple_of(lax.rem(block, per_part) * TILE, TILE)
    return ref.at[lax.div(block, per_part), :, pl.ds(lanes, TILE)]


def quantized(source, target, part, per_part):
    nvecs = source.shape[1]
    lane = lax.broadcasted_iota(jnp.int32, (nvecs, TILE), 1)
    exponents = jnp.zeros((nvecs, TILE), jnp.int32)
    for block in range(per_part):
        values = source[part, :, block * TILE : (block + 1) * TILE]
        largest = jnp.max(jnp.abs(values), axis=1, keepdims=True)
        power = jnp.floor(jnp.log2(jnp.maximum(largest, 2.0**-100)))
        scaled = jnp.round(values * jnp.exp2(14.0 - power))
        scaled = jnp.clip(scaled, -32767.0, 32767.0).astype(jnp.int32)
        target[part, :, block * TILE : (block + 1) * TILE] = scaled.astype(jnp.int16)
        exponents = jnp.where(lane == block, power.astype(jnp.int32), exponents)
    target[part, :, per_part * TILE :] = exponents.astype(jnp.int16)


def restored(source, part, block, per_part):
    exponents = source[part, :, per_part * TILE :].astype(jnp.int32).astype(jnp.float32)
    scale = jnp.exp2(exponents[:, block : block + 1] - 14.0)
    values = source[part, :, block * TILE : (block + 1) * TILE]
    return values.astype(jnp.int32).astype(jnp.float32) * scale


def tiles_kernel(transposed, per_part, meta, count, x_ref, stored_ref, out_ref, total, tiles_ref, arrived):
    live = count[0]
    groups = lax.div(live + UNROLL - 1, UNROLL)

    def fetched(index):
        part = pl.ds(index * UNROLL, UNROLL)
        return pltpu.make_async_copy(stored_ref.at[part], tiles_ref.at[part], arrived.at[index])

    def start(index, carry):
        fetched(index).start()
        return carry

    lax.fori_loop(0, groups, start, 0)
    nvecs = x_ref.shape[1]
    total[...] = jnp.zeros_like(total)
    lane = lax.broadcasted_iota(jnp.int32, (nvecs, TILE), 1)
    source, target = (1, 0) if transposed else (0, 1)

    def group(index, carry):
        fetched(index).wait()
        products = []
        for step in range(UNROLL):
            slot = index * UNROLL + step
            alive = slot < live
            code = meta[slot]
            blocks = (code & 0x7F, (code >> 7) & 0x7F)
            widths = [jnp.where(alive, (code >> shift) & 0xFF, 0) for shift in (14, 22)]
            taken, given = widths[source], widths[target]
            x = block_at(x_ref, blocks[source], per_part)[...]
            x = jnp.where(lane < taken, x.astype(jnp.float32), 0.0).astype(jnp.bfloat16)
            dims = (((1,), (1 if transposed else 0,)), ((), ()))
            product = lax.dot_general(x, tiles_ref[slot], dims, preferred_element_type=jnp.float32)
            products.append((blocks[target], jnp.where(lane < given, product, 0.0)))
        for block, product in products:
            block_at(total, block, per_part)[...] += product
        return carry

    lax.fori_loop(0, groups, group, 0)

    def part_out(part, carry):
        quantized(total, out_ref, part, per_part)
        return carry

    lax.fori_loop(0, out_ref.shape[0], part_out, 0)


def partials(transposed, meta, count, x, tiles):
    parts, nvecs, width = x.shape
    return pl.pallas_call(
        functools.partial(tiles_kernel, transposed, width // TILE),
        out_shape=jax.ShapeDtypeStruct((parts, nvecs, width + TILE), jnp.int16),
        in_specs=[SMEM, SMEM, VMEM, HBM],
        out_specs=VMEM,
        scratch_shapes=[
            pltpu.VMEM((parts, nvecs, width), jnp.float32),
            pltpu.VMEM(tiles.shape, tiles.dtype),
            pltpu.SemaphoreType.DMA((tiles.shape[0] // UNROLL,)),
        ],
        compiler_params=params(48),
        cost_estimate=pl.CostEstimate(flops=10**9, bytes_accessed=12 * 2**20, transcendentals=0),
    )(meta, count, x, tiles)


column_partials = functools.partial(partials, False)
row_partials = functools.partial(partials, True)


def summed_kernel(per_part, count, *refs):
    out_ref = refs[count]
    total_ref = out_ref if out_ref.dtype == jnp.float32 else refs[count + 1]
    for block in range(per_part):
        terms = [restored(ref, part, block, per_part) for ref in refs[:count] for part in range(ref.shape[0])]
        total = terms[0]
        for term in terms[1:]:
            total = total + term
        total_ref[0, :, block * TILE : (block + 1) * TILE] = total
    if total_ref is not out_ref:
        quantized(total_ref, out_ref, 0, per_part)


def summed(*parts, packed=False):
    _, nvecs, packed_width = parts[0].shape
    width = packed_width - TILE
    shape = (1, nvecs, packed_width if packed else width)
    return pl.pallas_call(
        functools.partial(summed_kernel, width // TILE, len(parts)),
        out_shape=jax.ShapeDtypeStruct(shape, jnp.int16 if packed else jnp.float32),
        in_specs=[VMEM] * len(parts),
        out_specs=VMEM,
        scratch_shapes=[pltpu.VMEM((1, nvecs, width), jnp.float32)] if packed else [],
        compiler_params=params(16),
    )(*parts)


def joined_kernel(per_part, rows_ref, arrived_ref, out_ref, total_ref):
    def one_part(part, carry):
        for block in range(per_part):
            lanes = slice(block * TILE, (block + 1) * TILE)
            total_ref[part, :, lanes] = restored(rows_ref, part, block, per_part) + restored(arrived_ref, part, block, per_part)
        quantized(total_ref, out_ref, part, per_part)
        return carry

    lax.fori_loop(0, out_ref.shape[0], one_part, 0)


def joined(rows, arrived):
    parts, nvecs, width = rows.shape[0], rows.shape[1], rows.shape[2] - TILE
    return pl.pallas_call(
        functools.partial(joined_kernel, width // TILE),
        out_shape=jax.ShapeDtypeStruct(arrived.shape, jnp.int16),
        in_specs=[VMEM, VMEM],
        out_specs=VMEM,
        scratch_shapes=[pltpu.VMEM((parts, nvecs, width), jnp.float32)],
        compiler_params=params(16),
    )(rows, arrived)


def per_device(vectors, tile_blocks, tile_index, tile_live, tile_count):
    n_diag, n_off = lax.axis_size("diag"), lax.axis_size("off")
    at = lambda a, b: (a % n_diag) * n_off + b
    across = lambda a, b: ((a >> 1) ^ ((a + b) >> 1)) & 1
    other = lambda a, b: b ^ (n_off // 2) if across(a, b) else b
    devices = [(a, b) for a in range(n_diag) for b in range(n_off)]
    fetch = [(at(a + b, other(a, b)), at(a, b)) for a, b in devices]
    back = [(at(a, b), at(a + b, (b if (a + b) % 2 == 0 else 7 - b))) for a, b in devices]
    meta = tile_index[:, 0] | (tile_index[:, 1] << 7) | (tile_live[:, 0] << 14) | (tile_live[:, 1] << 22)
    copies = jnp.broadcast_to(vectors[None], (n_off, *vectors.shape))
    copies, meta = lax.optimization_barrier((copies, meta))
    x_rows = lax.all_to_all(copies, "off", 0, 0)
    x_columns = lax.ppermute(x_rows, AXES, fetch)
    columns = column_partials(meta, tile_count, x_rows, tile_blocks)
    arrived = lax.ppermute(columns, AXES, back)
    rows = row_partials(meta, tile_count, x_columns, tile_blocks)
    return summed(lax.all_to_all(joined(rows, arrived), "off", 0, 0))[0]


def solution(mesh):
    placed = (
        P(None, AXES),
        P(AXES, None, None),
        P(AXES, None),
        P(AXES, None),
        P(AXES),
    )
    return jax.shard_map(
        per_device, mesh=mesh, in_specs=placed, out_specs=P(None, AXES), check_vma=False
    )
```

```python
import functools

import jax
import jax.numpy as jnp
from jax import lax
from jax.experimental import pallas as pl
from jax.experimental.pallas import tpu as pltpu
from jax.sharding import PartitionSpec as P

AXES = ("diag", "off")
TILE = 128
UNROLL = 32
VMEM = pl.BlockSpec(memory_space=pltpu.VMEM)
HBM = pl.BlockSpec(memory_space=pltpu.HBM)
SMEM = pl.BlockSpec(memory_space=pltpu.SMEM)


def params(mib):
    return pltpu.CompilerParams(vmem_limit_bytes=mib * 2**20)


def block_at(ref, block, per_part):
    lanes = pl.multiple_of(lax.rem(block, per_part) * TILE, TILE)
    return ref.at[lax.div(block, per_part), :, pl.ds(lanes, TILE)]


def quantized(source, target, part, per_part):
    nvecs = source.shape[1]
    lane = lax.broadcasted_iota(jnp.int32, (nvecs, TILE), 1)
    exponents = jnp.zeros((nvecs, TILE), jnp.int32)
    for block in range(per_part):
        values = source[part, :, block * TILE : (block + 1) * TILE]
        largest = jnp.max(jnp.abs(values), axis=1, keepdims=True)
        power = jnp.floor(jnp.log2(jnp.maximum(largest, 2.0**-112)))
        scaled = jnp.round(values * jnp.exp2(14.0 - power))
        scaled = jnp.clip(scaled, -32767.0, 32767.0).astype(jnp.int32)
        target[part, :, block * TILE : (block + 1) * TILE] = scaled.astype(jnp.int16)
        exponents = jnp.where(lane == block, power.astype(jnp.int32), exponents)
    target[part, :, per_part * TILE :] = exponents.astype(jnp.int16)


def scales_of(source, part, per_part):
    return jnp.exp2(source[part, :, per_part * TILE :].astype(jnp.int32).astype(jnp.float32) - 14.0)


def restored(source, scales, part, block):
    values = source[part, :, block * TILE : (block + 1) * TILE]
    return values.astype(jnp.int32).astype(jnp.float32) * scales[:, block : block + 1]


def tiles_kernel(transposed, per_part, pieces, meta, count, x_ref, stored_ref, *refs):
    sent_refs, (total, tiles_ref, arrived) = refs[:pieces], refs[pieces:]
    live = count[0]
    groups = lax.div(live + UNROLL - 1, UNROLL)

    def fetched(index):
        part = pl.ds(index * UNROLL, UNROLL)
        return pltpu.make_async_copy(stored_ref.at[part], tiles_ref.at[part], arrived.at[index])

    def start(index, carry):
        fetched(index).start()
        return carry

    lax.fori_loop(0, groups, start, 0)
    nvecs = x_ref.shape[1]
    total[...] = jnp.zeros_like(total)
    lane = lax.broadcasted_iota(jnp.int32, (nvecs, TILE), 1)
    source, target = (1, 0) if transposed else (0, 1)

    def group(index, carry):
        fetched(index).wait()
        products = []
        for step in range(UNROLL):
            slot = index * UNROLL + step
            alive = slot < live
            code = meta[slot]
            blocks = (code & 0x7F, (code >> 7) & 0x7F)
            widths = [jnp.where(alive, (code >> shift) & 0xFF, 0) for shift in (14, 22)]
            taken, given = widths[source], widths[target]
            x = block_at(x_ref, blocks[source], per_part)[...]
            x = jnp.where(lane < taken, x.astype(jnp.float32), 0.0).astype(jnp.bfloat16)
            dims = (((1,), (1 if transposed else 0,)), ((), ()))
            product = lax.dot_general(x, tiles_ref[slot], dims, preferred_element_type=jnp.float32)
            products.append((blocks[target], jnp.where(lane < given, product, 0.0)))
        for block, product in products:
            block_at(total, block, per_part)[...] += product
        return carry

    lax.fori_loop(0, groups, group, 0)
    if sent_refs:
        count_sent = total.shape[0] // len(sent_refs)
        for first, sent_ref in enumerate(sent_refs):

            def part_out(part, carry):
                quantized(total.at[pl.ds(first * count_sent, count_sent)], sent_ref, part, per_part)
                return carry

            lax.fori_loop(0, count_sent, part_out, 0)


def partials(transposed, pieces, meta, count, x, tiles):
    parts, nvecs, width = x.shape
    total = (parts, nvecs, width)
    if pieces:
        out_shape = [jax.ShapeDtypeStruct((parts // pieces, nvecs, width + TILE), jnp.int16)] * pieces
    else:
        out_shape = [jax.ShapeDtypeStruct(total, jnp.float32)]
    return pl.pallas_call(
        functools.partial(tiles_kernel, transposed, width // TILE, pieces),
        out_shape=out_shape,
        in_specs=[SMEM, SMEM, VMEM, HBM],
        out_specs=[VMEM] * len(out_shape),
        scratch_shapes=[pltpu.VMEM(total, jnp.float32)] * (1 if pieces else 0)
        + [
            pltpu.VMEM(tiles.shape, tiles.dtype),
            pltpu.SemaphoreType.DMA((tiles.shape[0] // UNROLL,)),
        ],
        compiler_params=params(48),
        cost_estimate=pl.CostEstimate(flops=10**9, bytes_accessed=12 * 2**20, transcendentals=0),
    )(meta, count, x, tiles)


def summed_kernel(per_part, count, *refs):
    out_ref = refs[count]
    total_ref = out_ref if out_ref.dtype == jnp.float32 else refs[count + 1]
    parts = [(ref, scales_of(ref, part, per_part), part) for ref in refs[:count] for part in range(ref.shape[0])]
    for block in range(per_part):
        terms = [restored(ref, scales, part, block) for ref, scales, part in parts]
        total = terms[0]
        for term in terms[1:]:
            total = total + term
        total_ref[0, :, block * TILE : (block + 1) * TILE] = total
    if total_ref is not out_ref:
        quantized(total_ref, out_ref, 0, per_part)


def summed(*parts, packed=False):
    _, nvecs, packed_width = parts[0].shape
    width = packed_width - TILE
    shape = (1, nvecs, packed_width if packed else width)
    return pl.pallas_call(
        functools.partial(summed_kernel, width // TILE, len(parts)),
        out_shape=jax.ShapeDtypeStruct(shape, jnp.int16 if packed else jnp.float32),
        in_specs=[VMEM] * len(parts),
        out_specs=VMEM,
        scratch_shapes=[pltpu.VMEM((1, nvecs, width), jnp.float32)] if packed else [],
        compiler_params=params(16),
    )(*parts)


def joined_kernel(per_part, rows_ref, *refs):
    arrived_refs, out_ref, total_ref = refs[:-2], refs[-2], refs[-1]
    each = arrived_refs[0].shape[0]
    for first, arrived_ref in enumerate(arrived_refs):

        def one_part(part, carry):
            whole = first * each + part
            scales = scales_of(arrived_ref, part, per_part)
            for block in range(per_part):
                lanes = slice(block * TILE, (block + 1) * TILE)
                total_ref[whole, :, lanes] = rows_ref[whole, :, lanes] + restored(arrived_ref, scales, part, block)
            quantized(total_ref, out_ref, whole, per_part)
            return carry

        lax.fori_loop(0, each, one_part, 0)


def joined(rows, *arrived):
    parts, nvecs, width = rows.shape
    return pl.pallas_call(
        functools.partial(joined_kernel, width // TILE),
        out_shape=jax.ShapeDtypeStruct((parts, nvecs, width + TILE), jnp.int16),
        in_specs=[VMEM] * (1 + len(arrived)),
        out_specs=VMEM,
        scratch_shapes=[pltpu.VMEM((parts, nvecs, width), jnp.float32)],
        compiler_params=params(16),
    )(rows, *arrived)


def per_device(vectors, tile_blocks, tile_index, tile_live, tile_count):
    n_diag, n_off = lax.axis_size("diag"), lax.axis_size("off")
    at = lambda a, b: (a % n_diag) * n_off + b
    across = lambda a, b: ((a >> 1) ^ ((a + b) >> 1)) & 1
    devices = [(a, b) for a in range(n_diag) for b in range(n_off)]
    fetch = [(at(a + b, b ^ (n_off // 2) if across(a, b) else b), at(a, b)) for a, b in devices]
    homes = [lambda c, b: b ^ 6, lambda c, b: b]
    copies = jnp.broadcast_to(vectors[None], (n_off, *vectors.shape))
    x_rows = lax.all_to_all(copies, "off", 0, 0)
    x_rows, tile_index, tile_live = lax.optimization_barrier((x_rows, tile_index, tile_live))
    meta = tile_index[:, 0] | (tile_index[:, 1] << 7) | (tile_live[:, 0] << 14) | (tile_live[:, 1] << 22)
    x_columns = lax.ppermute(x_rows, AXES, fetch)
    columns = partials(False, len(homes), meta, tile_count, x_rows, tile_blocks)
    arrived = [
        lax.ppermute(piece, AXES, [(at(a, b), at(a + b, home(a + b, b))) for a, b in devices])
        for piece, home in zip(columns, homes)
    ]
    (rows,) = partials(True, 0, meta, tile_count, x_columns, tile_blocks)
    return summed(lax.all_to_all(joined(rows, *arrived), "off", 0, 0))[0]


def solution(mesh):
    placed = (
        P(None, AXES),
        P(AXES, None, None),
        P(AXES, None),
        P(AXES, None),
        P(AXES),
    )
    return jax.shard_map(
        per_device, mesh=mesh, in_specs=placed, out_specs=P(None, AXES), check_vma=False
    )
```

```python
import functools

import jax
import jax.numpy as jnp
from jax import lax
from jax.experimental import pallas as pl
from jax.experimental.pallas import tpu as pltpu
from jax.sharding import PartitionSpec as P

AXES = ("diag", "off")
TILE = 128
UNROLL = 32
VMEM = pl.BlockSpec(memory_space=pltpu.VMEM)
HBM = pl.BlockSpec(memory_space=pltpu.HBM)
SMEM = pl.BlockSpec(memory_space=pltpu.SMEM)


def params(mib):
    return pltpu.CompilerParams(vmem_limit_bytes=mib * 2**20)


def block_at(ref, block, per_part):
    lanes = pl.multiple_of(lax.rem(block, per_part) * TILE, TILE)
    return ref.at[lax.div(block, per_part), :, pl.ds(lanes, TILE)]


def quantized(source, target, part, per_part):
    nvecs = source.shape[1]
    lane = lax.broadcasted_iota(jnp.int32, (nvecs, TILE), 1)
    exponents = jnp.zeros((nvecs, TILE), jnp.int32)
    for block in range(per_part):
        values = source[part, :, block * TILE : (block + 1) * TILE]
        largest = jnp.max(jnp.abs(values), axis=1, keepdims=True)
        power = jnp.floor(jnp.log2(jnp.maximum(largest, 2.0**-112)))
        scaled = jnp.round(values * jnp.exp2(14.0 - power))
        scaled = jnp.clip(scaled, -32767.0, 32767.0).astype(jnp.int32)
        target[part, :, block * TILE : (block + 1) * TILE] = scaled.astype(jnp.int16)
        exponents = jnp.where(lane == block, power.astype(jnp.int32), exponents)
    target[part, :, per_part * TILE :] = exponents.astype(jnp.int16)


def scales_of(source, part, per_part):
    return jnp.exp2(source[part, :, per_part * TILE :].astype(jnp.int32).astype(jnp.float32) - 14.0)


def restored(source, scales, part, block):
    values = source[part, :, block * TILE : (block + 1) * TILE]
    return values.astype(jnp.int32).astype(jnp.float32) * scales[:, block : block + 1]


def tiles_kernel(transposed, per_part, pieces, meta, count, x_ref, stored_ref, *refs):
    sent_refs, (total, tiles_ref, arrived) = refs[:pieces], refs[pieces:]
    live = count[0]
    groups = lax.div(live + UNROLL - 1, UNROLL)

    def fetched(index):
        part = pl.ds(index * UNROLL, UNROLL)
        return pltpu.make_async_copy(stored_ref.at[part], tiles_ref.at[part], arrived.at[index])

    def start(index, carry):
        fetched(index).start()
        return carry

    lax.fori_loop(0, groups, start, 0)
    nvecs = x_ref.shape[1]
    total[...] = jnp.zeros_like(total)
    lane = lax.broadcasted_iota(jnp.int32, (nvecs, TILE), 1)
    source, target = (1, 0) if transposed else (0, 1)

    def group(index, carry):
        fetched(index).wait()
        products = []
        for step in range(UNROLL):
            slot = index * UNROLL + step
            alive = slot < live
            code = meta[slot]
            blocks = (code & 0x7F, (code >> 7) & 0x7F)
            widths = [jnp.where(alive, (code >> shift) & 0xFF, 0) for shift in (14, 22)]
            taken, given = widths[source], widths[target]
            x = block_at(x_ref, blocks[source], per_part)[...]
            x = jnp.where(lane < taken, x.astype(jnp.float32), 0.0).astype(jnp.bfloat16)
            dims = (((1,), (1 if transposed else 0,)), ((), ()))
            product = lax.dot_general(x, tiles_ref[slot], dims, preferred_element_type=jnp.float32)
            products.append((blocks[target], jnp.where(lane < given, product, 0.0)))
        for block, product in products:
            block_at(total, block, per_part)[...] += product
        return carry

    lax.fori_loop(0, groups, group, 0)
    if sent_refs:
        count_sent = total.shape[0] // len(sent_refs)
        for first, sent_ref in enumerate(sent_refs):

            def part_out(part, carry):
                quantized(total.at[pl.ds(first * count_sent, count_sent)], sent_ref, part, per_part)
                return carry

            lax.fori_loop(0, count_sent, part_out, 0)


def partials(transposed, pieces, meta, count, x, tiles):
    parts, nvecs, width = x.shape
    total = (parts, nvecs, width)
    if pieces:
        out_shape = [jax.ShapeDtypeStruct((parts // pieces, nvecs, width + TILE), jnp.int16)] * pieces
    else:
        out_shape = [jax.ShapeDtypeStruct(total, jnp.float32)]
    return pl.pallas_call(
        functools.partial(tiles_kernel, transposed, width // TILE, pieces),
        out_shape=out_shape,
        in_specs=[SMEM, SMEM, VMEM, HBM],
        out_specs=[VMEM] * len(out_shape),
        scratch_shapes=[pltpu.VMEM(total, jnp.float32)] * (1 if pieces else 0)
        + [
            pltpu.VMEM(tiles.shape, tiles.dtype),
            pltpu.SemaphoreType.DMA((tiles.shape[0] // UNROLL,)),
        ],
        compiler_params=params(48),
        cost_estimate=pl.CostEstimate(flops=10**9, bytes_accessed=12 * 2**20, transcendentals=0),
    )(meta, count, x, tiles)


def summed_kernel(per_part, count, *refs):
    out_ref = refs[count]
    total_ref = out_ref if out_ref.dtype == jnp.float32 else refs[count + 1]
    parts = [(ref, scales_of(ref, part, per_part), part) for ref in refs[:count] for part in range(ref.shape[0])]
    for block in range(per_part):
        terms = [restored(ref, scales, part, block) for ref, scales, part in parts]
        total = terms[0]
        for term in terms[1:]:
            total = total + term
        total_ref[0, :, block * TILE : (block + 1) * TILE] = total
    if total_ref is not out_ref:
        quantized(total_ref, out_ref, 0, per_part)


def summed(*parts, packed=False):
    _, nvecs, packed_width = parts[0].shape
    width = packed_width - TILE
    shape = (1, nvecs, packed_width if packed else width)
    return pl.pallas_call(
        functools.partial(summed_kernel, width // TILE, len(parts)),
        out_shape=jax.ShapeDtypeStruct(shape, jnp.int16 if packed else jnp.float32),
        in_specs=[VMEM] * len(parts),
        out_specs=VMEM,
        scratch_shapes=[pltpu.VMEM((1, nvecs, width), jnp.float32)] if packed else [],
        compiler_params=params(16),
    )(*parts)


def joined_kernel(per_part, rows_ref, *refs):
    arrived_refs, out_ref, total_ref = refs[:-2], refs[-2], refs[-1]
    each = arrived_refs[0].shape[0]
    for first, arrived_ref in enumerate(arrived_refs):

        def one_part(part, carry):
            whole = first * each + part
            scales = scales_of(arrived_ref, part, per_part)
            for block in range(per_part):
                lanes = slice(block * TILE, (block + 1) * TILE)
                total_ref[whole, :, lanes] = rows_ref[whole, :, lanes] + restored(arrived_ref, scales, part, block)
            quantized(total_ref, out_ref, whole, per_part)
            return carry

        lax.fori_loop(0, each, one_part, 0)


def joined(rows, *arrived):
    parts, nvecs, width = rows.shape
    return pl.pallas_call(
        functools.partial(joined_kernel, width // TILE),
        out_shape=jax.ShapeDtypeStruct((parts, nvecs, width + TILE), jnp.int16),
        in_specs=[VMEM] * (1 + len(arrived)),
        out_specs=VMEM,
        scratch_shapes=[pltpu.VMEM((parts, nvecs, width), jnp.float32)],
        compiler_params=params(16),
    )(rows, *arrived)


def per_device(vectors, tile_blocks, tile_index, tile_live, tile_count):
    n_diag, n_off = lax.axis_size("diag"), lax.axis_size("off")
    at = lambda a, b: (a % n_diag) * n_off + b
    across = lambda a, b: ((a >> 1) ^ ((a + b) >> 1)) & 1
    devices = [(a, b) for a in range(n_diag) for b in range(n_off)]
    fetch = [(at(a + b, b ^ (n_off // 2) if across(a, b) else b), at(a, b)) for a, b in devices]
    homes = [lambda c, b: b ^ 6, lambda c, b: b ^ 4]
    copies = jnp.broadcast_to(vectors[None], (n_off, *vectors.shape))
    x_rows = lax.all_to_all(copies, "off", 0, 0)
    x_rows, tile_index, tile_live = lax.optimization_barrier((x_rows, tile_index, tile_live))
    meta = tile_index[:, 0] | (tile_index[:, 1] << 7) | (tile_live[:, 0] << 14) | (tile_live[:, 1] << 22)
    x_columns = lax.ppermute(x_rows, AXES, fetch)
    columns = partials(False, len(homes), meta, tile_count, x_rows, tile_blocks)
    arrived = [
        lax.ppermute(piece, AXES, [(at(a, b), at(a + b, home(a + b, b))) for a, b in devices])
        for piece, home in zip(columns, homes)
    ]
    (rows,) = partials(True, 0, meta, tile_count, x_columns, tile_blocks)
    return summed(lax.all_to_all(joined(rows, *arrived), "off", 0, 0))[0]


def solution(mesh):
    placed = (
        P(None, AXES),
        P(AXES, None, None),
        P(AXES, None),
        P(AXES, None),
        P(AXES),
    )
    return jax.shard_map(
        per_device, mesh=mesh, in_specs=placed, out_specs=P(None, AXES), check_vma=False
    )
```

```python
import functools

import jax
import jax.numpy as jnp
from jax import lax
from jax.experimental import pallas as pl
from jax.experimental.pallas import tpu as pltpu
from jax.sharding import PartitionSpec as P

AXES = ("diag", "off")
TILE = 128
UNROLL = 32
VMEM = pl.BlockSpec(memory_space=pltpu.VMEM)
HBM = pl.BlockSpec(memory_space=pltpu.HBM)
SMEM = pl.BlockSpec(memory_space=pltpu.SMEM)


def params(mib):
    return pltpu.CompilerParams(vmem_limit_bytes=mib * 2**20)


def block_at(ref, block, per_part):
    lanes = pl.multiple_of(lax.rem(block, per_part) * TILE, TILE)
    return ref.at[lax.div(block, per_part), :, pl.ds(lanes, TILE)]


def quantized(source, target, part, per_part):
    nvecs = source.shape[1]
    lane = lax.broadcasted_iota(jnp.int32, (nvecs, TILE), 1)
    exponents = jnp.zeros((nvecs, TILE), jnp.int32)
    for block in range(per_part):
        values = source[part, :, block * TILE : (block + 1) * TILE]
        largest = jnp.max(jnp.abs(values), axis=1, keepdims=True)
        power = jnp.floor(jnp.log2(jnp.maximum(largest, 2.0**-112)))
        scaled = jnp.round(values * jnp.exp2(14.0 - power))
        scaled = jnp.minimum(scaled, 32767.0).astype(jnp.int32)
        target[part, :, block * TILE : (block + 1) * TILE] = scaled.astype(jnp.int16)
        exponents = jnp.where(lane == block, power.astype(jnp.int32), exponents)
    target[part, :, per_part * TILE :] = exponents.astype(jnp.int16)


def scales_of(source, part, per_part):
    return jnp.exp2(source[part, :, per_part * TILE :].astype(jnp.int32).astype(jnp.float32) - 14.0)


def restored(source, scales, part, block):
    values = source[part, :, block * TILE : (block + 1) * TILE]
    return values.astype(jnp.int32).astype(jnp.float32) * scales[:, block : block + 1]


def tiles_kernel(transposed, per_part, pieces, meta, count, x_ref, stored_ref, *refs):
    sent_refs, (total, tiles_ref, arrived) = refs[:pieces], refs[pieces:]
    live = count[0]
    groups = lax.div(live + UNROLL - 1, UNROLL)

    def fetched(index):
        part = pl.ds(index * UNROLL, UNROLL)
        return pltpu.make_async_copy(stored_ref.at[part], tiles_ref.at[part], arrived.at[index])

    def start(index, carry):
        fetched(index).start()
        return carry

    lax.fori_loop(0, groups, start, 0)
    nvecs = x_ref.shape[1]
    total[...] = jnp.zeros_like(total)
    lane = lax.broadcasted_iota(jnp.int32, (nvecs, TILE), 1)
    source, target = (1, 0) if transposed else (0, 1)

    def group(index, carry):
        fetched(index).wait()
        products = []
        for step in range(UNROLL):
            slot = index * UNROLL + step
            alive = slot < live
            code = meta[slot]
            blocks = (code & 0x7F, (code >> 7) & 0x7F)
            widths = [jnp.where(alive, (code >> shift) & 0xFF, 0) for shift in (14, 22)]
            taken, given = widths[source], widths[target]
            x = block_at(x_ref, blocks[source], per_part)[...]
            x = jnp.where(lane < taken, x.astype(jnp.float32), 0.0).astype(jnp.bfloat16)
            dims = (((1,), (1 if transposed else 0,)), ((), ()))
            product = lax.dot_general(x, tiles_ref[slot], dims, preferred_element_type=jnp.float32)
            products.append((blocks[target], jnp.where(lane < given, product, 0.0)))
        for block, product in products:
            block_at(total, block, per_part)[...] += product
        return carry

    lax.fori_loop(0, groups, group, 0)
    if sent_refs:
        count_sent = total.shape[0] // len(sent_refs)
        for first, sent_ref in enumerate(sent_refs):

            def part_out(part, carry):
                quantized(total.at[pl.ds(first * count_sent, count_sent)], sent_ref, part, per_part)
                return carry

            lax.fori_loop(0, count_sent, part_out, 0, unroll=True)


def partials(transposed, pieces, meta, count, x, tiles):
    parts, nvecs, width = x.shape
    total = (parts, nvecs, width)
    if pieces:
        out_shape = [jax.ShapeDtypeStruct((parts // pieces, nvecs, width + TILE), jnp.int16)] * pieces
    else:
        out_shape = [jax.ShapeDtypeStruct(total, jnp.float32)]
    return pl.pallas_call(
        functools.partial(tiles_kernel, transposed, width // TILE, pieces),
        out_shape=out_shape,
        in_specs=[SMEM, SMEM, VMEM, HBM],
        out_specs=[VMEM] * len(out_shape),
        scratch_shapes=[pltpu.VMEM(total, jnp.float32)] * (1 if pieces else 0)
        + [
            pltpu.VMEM(tiles.shape, tiles.dtype),
            pltpu.SemaphoreType.DMA((tiles.shape[0] // UNROLL,)),
        ],
        compiler_params=params(48),
        cost_estimate=pl.CostEstimate(flops=10**9, bytes_accessed=12 * 2**20, transcendentals=0),
    )(meta, count, x, tiles)


def summed_kernel(per_part, count, *refs):
    out_ref = refs[count]
    total_ref = out_ref if out_ref.dtype == jnp.float32 else refs[count + 1]
    parts = [(ref, scales_of(ref, part, per_part), part) for ref in refs[:count] for part in range(ref.shape[0])]
    for block in range(per_part):
        terms = [restored(ref, scales, part, block) for ref, scales, part in parts]
        total = terms[0]
        for term in terms[1:]:
            total = total + term
        total_ref[0, :, block * TILE : (block + 1) * TILE] = total
    if total_ref is not out_ref:
        quantized(total_ref, out_ref, 0, per_part)


def summed(*parts, packed=False):
    _, nvecs, packed_width = parts[0].shape
    width = packed_width - TILE
    shape = (1, nvecs, packed_width if packed else width)
    return pl.pallas_call(
        functools.partial(summed_kernel, width // TILE, len(parts)),
        out_shape=jax.ShapeDtypeStruct(shape, jnp.int16 if packed else jnp.float32),
        in_specs=[VMEM] * len(parts),
        out_specs=VMEM,
        scratch_shapes=[pltpu.VMEM((1, nvecs, width), jnp.float32)] if packed else [],
        compiler_params=params(16),
    )(*parts)


def joined_kernel(per_part, rows_ref, *refs):
    arrived_refs, out_ref, total_ref = refs[:-2], refs[-2], refs[-1]
    each = arrived_refs[0].shape[0]
    for first, arrived_ref in enumerate(arrived_refs):

        def one_part(part, carry):
            whole = first * each + part
            scales = scales_of(arrived_ref, part, per_part)
            for block in range(per_part):
                lanes = slice(block * TILE, (block + 1) * TILE)
                total_ref[whole, :, lanes] = rows_ref[whole, :, lanes] + restored(arrived_ref, scales, part, block)
            quantized(total_ref, out_ref, whole, per_part)
            return carry

        lax.fori_loop(0, each, one_part, 0, unroll=True)


def joined(rows, *arrived):
    parts, nvecs, width = rows.shape
    return pl.pallas_call(
        functools.partial(joined_kernel, width // TILE),
        out_shape=jax.ShapeDtypeStruct((parts, nvecs, width + TILE), jnp.int16),
        in_specs=[VMEM] * (1 + len(arrived)),
        out_specs=VMEM,
        scratch_shapes=[pltpu.VMEM((parts, nvecs, width), jnp.float32)],
        compiler_params=params(16),
    )(rows, *arrived)


def per_device(vectors, tile_blocks, tile_index, tile_live, tile_count):
    n_diag, n_off = lax.axis_size("diag"), lax.axis_size("off")
    at = lambda a, b: (a % n_diag) * n_off + b
    across = lambda a, b: ((a >> 1) ^ ((a + b) >> 1)) & 1
    devices = [(a, b) for a in range(n_diag) for b in range(n_off)]
    fetch = [(at(a + b, b ^ (n_off // 2) if across(a, b) else b), at(a, b)) for a, b in devices]
    homes = [lambda c, b: b ^ 6, lambda c, b: b ^ 4]
    copies = jnp.broadcast_to(vectors[None], (n_off, *vectors.shape))
    x_rows = lax.all_to_all(copies, "off", 0, 0)
    x_rows, tile_index, tile_live = lax.optimization_barrier((x_rows, tile_index, tile_live))
    meta = tile_index[:, 0] | (tile_index[:, 1] << 7) | (tile_live[:, 0] << 14) | (tile_live[:, 1] << 22)
    x_columns = lax.ppermute(x_rows, AXES, fetch)
    columns = partials(False, len(homes), meta, tile_count, x_rows, tile_blocks)
    arrived = [
        lax.ppermute(piece, AXES, [(at(a, b), at(a + b, home(a + b, b))) for a, b in devices])
        for piece, home in zip(columns, homes)
    ]
    (rows,) = partials(True, 0, meta, tile_count, x_columns, tile_blocks)
    return summed(lax.all_to_all(joined(rows, *arrived), "off", 0, 0))[0]


def solution(mesh):
    placed = (
        P(None, AXES),
        P(AXES, None, None),
        P(AXES, None),
        P(AXES, None),
        P(AXES),
    )
    return jax.shard_map(
        per_device, mesh=mesh, in_specs=placed, out_specs=P(None, AXES), check_vma=False
    )
```
